32 devices in a mesh: rep: 8 (over z, y), shard: 4 (over x, core).
Axes of the slice: x: 2, y: 2, z: 4, core: 2. Of those that a mesh axis runs over, the one named last changes fastest.
Arguments:
- gradient: bfloat16 [8, 1024, 4096], P('rep', None, 'shard'), may hold values from -16 to 16
- feedback: bfloat16 [8, 1024, 4096], P('rep', None, 'shard'), may hold values from -4 to 4
- warm_start: float32 [1024, 64], replicated, may hold values from -6 to 6
- master: float32 [1024, 4096], P('rep', 'shard'), may hold values from -4 to 4
- moment: float32 [1024, 4096], P('rep', 'shard'), may hold values from -1.5 to 1.5
- second: float32 [1024, 4096], P('rep', 'shard'), may hold values from 0.005 to 0.5
Outputs:
- new_feedback: bfloat16 [8, 1024, 4096], P('rep', None, 'shard')
- weights: bfloat16 [1024, 4096], P(None, 'shard')
- master_out: float32 [1024, 4096], P('rep', 'shard')
- moment_out: float32 [1024, 4096], P('rep', 'shard')
- second_out: float32 [1024, 4096], P('rep', 'shard')
- right_factor: float32 [1024, 64], replicated
The draws below stay inside these ranges and needn't reach their ends.
All inputs are finite; a program needn't handle non-finite values.
Results may differ from the reference program's by a relative error of at most 0.001.
Values may be sent and summed in bfloat16 or wider, within the bound.
A program may use at most 64 MiB of HBM per device.

```python
import math
import jax
import jax.numpy as jnp
from jax import lax

FF = 4096
DW = 1024
RANK = 64
REPLICAS = 8


def draw_gradient(key, part):
    key_cols, key_rows, key_own = jax.random.split(key, 3)
    column_pos = jnp.arange(FF, dtype=jnp.float32) / FF
    replica_pos = jnp.arange(REPLICAS, dtype=jnp.float32) / REPLICAS
    column_scale = jnp.exp(jax.random.uniform(key_cols, (FF,), jnp.float32, 0.0, math.log(10.0)))
    row_scale = jnp.exp(jax.random.uniform(key_rows, (DW,), jnp.float32, 0.0, math.log(4.0)))
    values = jax.random.truncated_normal(key_own, -4.0, 4.0, (REPLICAS, DW, FF), jnp.float32)
    rising = jnp.power(3.0, 0.5 * column_pos)
    base_scale = 0.06
    scale_all = base_scale * (column_scale * rising)[None, None, :] * row_scale[None, :, None]
    scale_all = scale_all * jnp.power(3.0, 0.5 * replica_pos)[:, None, None]
    return jnp.clip(values * scale_all, -16.0, 16.0).astype(jnp.bfloat16)


def block_levels(stream_key, extent, cuts, least, high):
    def one(position, shards_of):
        draws = jax.random.uniform(jax.random.fold_in(jax.random.fold_in(stream_key, 6), position), (shards_of,), jnp.float32, least / len(cuts), high / len(cuts))
        return jnp.repeat(jnp.exp(draws), extent[position] // shards_of).reshape((-1,) + (1,) * (len(extent) - position - 1))

    factor_of = one(*cuts[0])
    for cut in cuts[1:]:
        factor_of = factor_of * one(*cut)
    return factor_of


def gaussian(stream_key, dims, width, most, shards=(), kind=jnp.bfloat16):
    entries = width * jax.random.normal(stream_key, dims, jnp.float32)
    if shards:
        entries = entries * block_levels(stream_key, dims, shards, -0.22, 0.18)
    return jnp.clip(entries, -most, most).astype(kind)


def setup_inputs(seed: int = 0) -> dict:
    keys = jax.random.split(jax.random.key(seed), 7)
    return {
        "gradient": draw_gradient(jax.random.fold_in(keys[6], 71), 0),
        "feedback": gaussian(keys[1], (REPLICAS, DW, FF), 0.5, 4.0, ((0, 8), (2, 4))),
        "warm_start": gaussian(keys[2], (DW, RANK), 1.0, 6.0, (), jnp.float32),
        "master": gaussian(keys[3], (DW, FF), 1.0, 4.0, ((0, 8), (1, 4)), jnp.float32),
        "moment": gaussian(keys[4], (DW, FF), 0.1, 1.5, ((0, 8), (1, 4)), jnp.float32),
        "second": jnp.clip(jnp.exp(math.log(0.5) - 4.6051702 * jax.random.uniform(keys[5], (DW, FF), jnp.float32) ** block_levels(keys[5], (DW, FF), ((0, 8), (1, 4)), -0.2, 0.2)), 0.005, 0.5),
    }


HIGHEST = lax.Precision.HIGHEST
beta_one = 0.9
beta_two = 0.95
learn_rate = 0.02
decay_rate = 0.1
adam_eps = 1e-08
ridge_rate = 1e-06

def lower_inverse(gram):
    matrix_order = gram.shape[0]
    identity = jnp.eye(matrix_order, dtype=jnp.float32)
    ridge_term = ridge_rate * jnp.trace(gram) / matrix_order
    cholesky_lower = jnp.linalg.cholesky(gram + ridge_term * identity)
    return jax.scipy.linalg.solve_triangular(cholesky_lower, identity, lower=True)

def contract_first(left, right):
    return lax.dot_general(left.astype(jnp.float32), right.astype(jnp.float32), (((0,), (0,)), ((), ())), precision=HIGHEST, preferred_element_type=jnp.float32)

def reference(gradient, feedback, warm_start, master, moment, second):
    replicas = gradient.shape[0]

    def factor_step(running, slices):
        merged = slices[0].astype(jnp.float32) + slices[1].astype(jnp.float32)
        return (running + contract_first(merged, warm_start), None)
    zero_factor = jnp.zeros((gradient.shape[2], warm_start.shape[1]), jnp.float32)
    factor, _ = lax.scan(factor_step, zero_factor, (gradient, feedback))
    factor = factor / replicas
    gram = contract_first(factor, factor)
    inverse = lower_inverse(gram)
    unit_basis = jnp.dot(factor.astype(jnp.float32), inverse.T.astype(jnp.float32), precision=HIGHEST, preferred_element_type=jnp.float32)

    def project_step(running, slices):
        merged = slices[0].astype(jnp.float32) + slices[1].astype(jnp.float32)
        return (running + jnp.dot(merged.astype(jnp.float32), unit_basis.astype(jnp.float32), precision=HIGHEST, preferred_element_type=jnp.float32), None)
    zero_right = jnp.zeros(warm_start.shape, jnp.float32)
    right_factor, _ = lax.scan(project_step, zero_right, (gradient, feedback))
    right_factor = right_factor / replicas
    approx = lax.dot_general(right_factor.astype(jnp.float32), unit_basis.astype(jnp.float32), (((1,), (1,)), ((), ())), precision=HIGHEST, preferred_element_type=jnp.float32)

    def residue(slices):
        merged = slices[0].astype(jnp.float32) + slices[1].astype(jnp.float32)
        return (merged - approx).astype(jnp.bfloat16)
    new_feedback = lax.map(residue, (gradient, feedback))
    moment_out = beta_one * moment + (1.0 - beta_one) * approx
    second_out = beta_two * second + (1.0 - beta_two) * approx * approx
    master_out = master - learn_rate * (moment_out / (jnp.sqrt(second_out) + adam_eps) + decay_rate * master)
    return (new_feedback, master_out.astype(jnp.bfloat16), master_out, moment_out, second_out, right_factor)
```

```python
import functools

import jax
import jax.numpy as jnp
from jax import lax
from jax.experimental import pallas as pl
from jax.experimental.pallas import tpu as pltpu
from jax.sharding import PartitionSpec as P

HIGHEST = lax.Precision.HIGHEST
MESH = pl.DeviceIdType.MESH
beta_one = 0.9
beta_two = 0.95
learn_rate = 0.02
decay_rate = 0.1
adam_eps = 1e-08
ridge_rate = 1e-06
bf16 = jnp.bfloat16
f32 = jnp.float32


def lower_inverse(gram, order):
    rows = lax.broadcasted_iota(jnp.int32, (order, order), 0)
    cols = lax.broadcasted_iota(jnp.int32, (order, order), 1)
    eye = (rows == cols).astype(f32)
    trace = jnp.sum(gram * eye, keepdims=True)
    work = jnp.concatenate([gram + (ridge_rate / order) * trace * eye, eye], axis=1)
    below = lax.broadcasted_iota(jnp.int32, (order, 1), 0)
    for j in range(order - 1):
        pivot_row = work[j : j + 1, :]
        column = work[:, j : j + 1] * (1.0 / work[j : j + 1, j : j + 1])
        work = work - jnp.where(below > j, column, 0.0) * pivot_row
    pivots = jnp.sum(work[:, :order] * eye, axis=1, keepdims=True)
    return work[:, order:] * (1.0 / jnp.sqrt(pivots))


def split(value):
    high = value.astype(bf16)
    return high, (value - high.astype(f32)).astype(bf16)


def nn(left, right):
    return jnp.dot(left, right, preferred_element_type=f32)


def nt(left, right, precision=None):
    return lax.dot_general(
        left, right, (((1,), (1,)), ((), ())), precision=precision, preferred_element_type=f32
    )


def kernel(
    reps, shards, inner,
    g_hbm, f_hbm, w_ref, master_hbm, moment_hbm, second_hbm,
    nf_hbm, wt_hbm, master_o, moment_o, second_o, right_o,
    gv, fv, w2, acc, ft, u3, state, apx,
    fsend, frecv, fall, grams, psend, precv, qx, rall, wall,
    load_sem, state_sem, f_ss, f_rs, a_ss, a_rs, gr_ss, gr_rs, p_ss, p_rs, q_ss, q_rs, r_ss, r_rs,
    w_ss, w_rs, nf_sem, wo_sem, so_sem, ro_sem,
):
    rank = w_ref.shape[1]
    depth, cols = gv.shape
    own_rows = state.shape[1]
    cb = fsend.shape[2]
    outer = reps // inner
    me = lax.axis_index("rep")
    ms = lax.axis_index("shard")
    chunks = load_sem.shape[1]
    crows = depth // chunks

    def load(c):
        part = pl.ds(c * crows, crows)
        return (
            pltpu.make_async_copy(g_hbm.at[0, part], gv.at[part], load_sem.at[0, c]),
            pltpu.make_async_copy(f_hbm.at[0, part], fv.at[part], load_sem.at[1, c]),
        )

    for c in range(chunks):
        for copy in load(c):
            copy.start()
    state_in = [
        pltpu.make_async_copy(src, state.at[i], state_sem.at[i])
        for i, src in enumerate((master_hbm, moment_hbm, second_hbm))
    ]
    for copy in state_in:
        copy.start()

    barrier = pltpu.get_barrier_semaphore()
    for k in range(1, reps):
        pl.semaphore_signal(barrier, inc=1, device_id={"rep": lax.rem(me + k, reps)}, device_id_type=MESH)
    for k in range(1, shards):
        pl.semaphore_signal(barrier, inc=1, device_id={"shard": lax.rem(ms + k, shards)}, device_id_type=MESH)

    def remote(src, dst, send_sem, recv_sem, axis, peer):
        return pltpu.make_async_remote_copy(
            src_ref=src, dst_ref=dst, send_sem=send_sem, recv_sem=recv_sem,
            device_id={axis: peer}, device_id_type=MESH,
        )

    wh, wl = split(w_ref[...].T)
    w2[...] = jnp.concatenate([wh, wl], axis=0)
    for c in range(chunks):
        for copy in load(c):
            copy.wait()
        part = pl.ds(c * crows, crows)
        term = nn(w2[:, part], gv[part, :]) + nn(w2[:, part], fv[part, :])
        if c == 0:
            acc[...] = term
        else:
            acc[...] += term
    for r in range(reps):
        part = pl.ds(r * cb, cb)
        fsend[r] = acc[:rank, part] + acc[rank:, part]
    pl.semaphore_wait(barrier, reps + shards - 2)

    def scatter(k):
        peer = lax.rem(me + k, reps)
        return remote(fsend.at[peer], frecv.at[k], f_ss.at[k], f_rs.at[k], "rep", peer)

    for k in range(1, reps):
        scatter(k).start()
    total = fsend[me]
    for k in range(1, reps):
        scatter(k).wait_recv()
        total = total + frecv[k]
    fall[me] = total * (1.0 / reps)

    def gather(buf, ss, rs, axis, size, mine, k, sending):
        peer = lax.rem(mine + k, size) if sending else lax.rem(mine + size - k, size)
        slot = mine if sending else peer
        return remote(buf.at[slot], buf.at[slot], ss.at[k], rs.at[k], axis, lax.rem(mine + k, size))

    def start_gather(buf, ss, rs, axis, size, mine):
        for k in range(1, size):
            gather(buf, ss, rs, axis, size, mine, k, True).start()

    def wait_gather(buf, ss, rs, axis, size, mine):
        for k in range(1, size):
            gather(buf, ss, rs, axis, size, mine, k, False).wait_recv()

    start_gather(fall, a_ss, a_rs, "rep", reps, me)
    wait_gather(fall, a_ss, a_rs, "rep", reps, me)
    for r in range(reps):
        ft[:, pl.ds(r * cb, cb)] = fall[r]
    factor = ft[...]
    grams[ms] = nt(factor, factor, HIGHEST)
    start_gather(grams, gr_ss, gr_rs, "shard", shards, ms)
    wait_gather(grams, gr_ss, gr_rs, "shard", shards, ms)
    gram = grams[0]
    for s in range(1, shards):
        gram = gram + grams[s]
    inverse = lower_inverse(gram, rank)
    basis = jnp.dot(inverse, ft[...], precision=HIGHEST, preferred_element_type=f32)
    uh, ul = split(basis)
    u3[...] = jnp.concatenate([uh, ul, uh], axis=0)

    def project(peer):
        part = pl.ds(pl.multiple_of(peer * own_rows, own_rows), own_rows)
        both = nt(u3[: 2 * rank, :], gv[part, :]) + nt(u3[: 2 * rank, :], fv[part, :])
        return both[:rank] + both[rank:]

    def scatter_right(k):
        peer = lax.rem(me + k, reps)
        return remote(psend.at[peer], precv.at[k], p_ss.at[k], p_rs.at[k], "rep", peer)

    for k in range(1, reps):
        peer = lax.rem(me + k, reps)
        psend[peer] = project(peer)
        scatter_right(k).start()
    total = project(me)
    for k in range(1, reps):
        scatter_right(k).wait_recv()
        total = total + precv[k]
    qx[ms] = total
    start_gather(qx, q_ss, q_rs, "shard", shards, ms)
    wait_gather(qx, q_ss, q_rs, "shard", shards, ms)
    total = qx[0]
    for s in range(1, shards):
        total = total + qx[s]
    rall[me] = total * (1.0 / reps)
    start_gather(rall, r_ss, r_rs, "rep", reps, me)

    def approx_rows(r):
        rh, rl = split(rall[r].T)
        return nn(jnp.concatenate([rh, rh, rl], axis=1), u3[...])

    apx[...] = approx_rows(me)
    for copy in state_in:
        copy.wait()
    step_rows = 16

    def adam(i, carry):
        part = pl.ds(pl.multiple_of(i * step_rows, step_rows), step_rows)
        grad = apx[part, :]
        master = state[0, part, :]
        moment_out = beta_one * state[1, part, :] + (1.0 - beta_one) * grad
        second_out = beta_two * state[2, part, :] + (1.0 - beta_two) * grad * grad
        master_out = master - learn_rate * (
            moment_out / (jnp.sqrt(second_out) + adam_eps) + decay_rate * master
        )
        state[0, part, :] = master_out
        state[1, part, :] = moment_out
        state[2, part, :] = second_out
        wall[me, part, :] = master_out.astype(bf16)
        return carry

    lax.fori_loop(0, own_rows // step_rows, adam, 0)

    ma = lax.div(me, inner)
    mb = lax.rem(me, inner)

    def hop(block, way, peer):
        return remote(wall.at[block], wall.at[block], w_ss.at[block, way], w_rs.at[block], "rep", peer)

    def forward(a, up, down):
        block = a * inner + mb
        if up:
            @pl.when(ma + 1 < outer)
            def _():
                hop(block, 0, me + inner).start()
        if down:
            @pl.when(ma > 0)
            def _():
                hop(block, 1, me - inner).start()
        for j in range(1, inner):
            hop(block, 1 + j, ma * inner + lax.rem(mb + j, inner)).start()

    def keep(block):
        part = pl.ds(pl.multiple_of(block * own_rows, own_rows), own_rows)
        return pltpu.make_async_copy(wall.at[block], wt_hbm.at[part], wo_sem.at[block])

    forward(ma, True, True)
    keep(me).start()
    state_out = [
        pltpu.make_async_copy(state.at[i], dst, so_sem.at[i])
        for i, dst in enumerate((master_o, moment_o, second_o))
    ]
    for copy in state_out:
        copy.start()

    wait_gather(rall, r_ss, r_rs, "rep", reps, me)
    right_copy = pltpu.make_async_copy(rall, right_o, ro_sem)
    right_copy.start()

    def residue(r):
        part = pl.ds(pl.multiple_of(r * own_rows, own_rows), own_rows)
        return part, pltpu.make_async_copy(gv.at[part], nf_hbm.at[0, part], nf_sem.at[r])

    def feedback_rows(r, carry):
        part, copy = residue(r)
        merged = gv[part, :].astype(f32) + fv[part, :].astype(f32)
        gv[part, :] = (merged - approx_rows(r)).astype(bf16)
        copy.start()
        return carry

    lax.fori_loop(0, reps, feedback_rows, 0)

    for t in range(1, outer):
        @pl.when(ma - t >= 0)
        def _():
            block = (ma - t) * inner + mb
            hop(block, 0, me).wait_recv()
            forward(ma - t, True, False)
            keep(block).start()

        @pl.when(ma + t < outer)
        def _():
            block = (ma + t) * inner + mb
            hop(block, 1, me).wait_recv()
            forward(ma + t, False, True)
            keep(block).start()

    for j in range(1, inner):
        for a in range(outer):
            block = a * inner + lax.rem(mb + j, inner)
            hop(block, 1 + j, me).wait_recv()
            keep(block).start()

    for k in range(1, reps):
        scatter(k).wait_send()
        scatter_right(k).wait_send()
        gather(fall, a_ss, a_rs, "rep", reps, me, k, True).wait_send()
        gather(rall, r_ss, r_rs, "rep", reps, me, k, True).wait_send()
    for k in range(1, shards):
        gather(grams, gr_ss, gr_rs, "shard", shards, ms, k, True).wait_send()
        gather(qx, q_ss, q_rs, "shard", shards, ms, k, True).wait_send()
    for a in range(outer):
        block = a * inner + mb

        @pl.when((a <= ma) & (ma + 1 < outer))
        def _():
            hop(block, 0, me).wait_send()

        @pl.when((a >= ma) & (ma > 0))
        def _():
            hop(block, 1, me).wait_send()

        for j in range(1, inner):
            hop(block, 1 + j, me).wait_send()
    for copy in state_out:
        copy.wait()
    right_copy.wait()
    for r in range(reps):
        residue(r)[1].wait()
        keep(r).wait()


def on_device(gradient, feedback, warm_start, master, moment, second):
    reps = lax.axis_size("rep")
    shards = lax.axis_size("shard")
    inner = 2 if reps <= 8 else 8
    _, depth, cols = gradient.shape
    rank = warm_start.shape[1]
    own_rows = master.shape[0]
    cb = cols // reps
    chunks = 4
    dma = pltpu.SemaphoreType.DMA
    anywhere = pl.BlockSpec(memory_space=pl.ANY)
    new_feedback, weights, master_out, moment_out, second_out, right = pl.pallas_call(
        functools.partial(kernel, reps, shards, inner),
        out_shape=(
            jax.ShapeDtypeStruct(gradient.shape, bf16),
            jax.ShapeDtypeStruct((depth, cols), bf16),
            jax.ShapeDtypeStruct(master.shape, f32),
            jax.ShapeDtypeStruct(master.shape, f32),
            jax.ShapeDtypeStruct(master.shape, f32),
            jax.ShapeDtypeStruct((reps, rank, own_rows), f32),
        ),
        in_specs=[anywhere, anywhere, pl.BlockSpec(memory_space=pltpu.VMEM)] + [anywhere] * 3,
        out_specs=(anywhere,) * 6,
        scratch_shapes=[
            pltpu.VMEM((depth, cols), bf16),
            pltpu.VMEM((depth, cols), bf16),
            pltpu.VMEM((2 * rank, depth), bf16),
            pltpu.VMEM((2 * rank, cols), f32),
            pltpu.VMEM((rank, cols), f32),
            pltpu.VMEM((3 * rank, cols), bf16),
            pltpu.VMEM((3, own_rows, cols), f32),
            pltpu.VMEM((own_rows, cols), f32),
            pltpu.VMEM((reps, rank, cb), f32),
            pltpu.VMEM((reps, rank, cb), f32),
            pltpu.VMEM((reps, rank, cb), f32),
            pltpu.VMEM((shards, rank, rank), f32),
            pltpu.VMEM((reps, rank, own_rows), f32),
            pltpu.VMEM((reps, rank, own_rows), f32),
            pltpu.VMEM((shards, rank, own_rows), f32),
            pltpu.VMEM((reps, rank, own_rows), f32),
            pltpu.VMEM((reps, own_rows, cols), bf16),
            dma((2, chunks)),
            dma((3,)),
            dma((reps,)), dma((reps,)),
            dma((reps,)), dma((reps,)),
            dma((shards,)), dma((shards,)),
            dma((reps,)), dma((reps,)),
            dma((shards,)), dma((shards,)),
            dma((reps,)), dma((reps,)),
            dma((reps, inner + 1)), dma((reps,)),
            dma((reps,)), dma((reps,)), dma((3,)), dma(()),
        ],
        compiler_params=pltpu.CompilerParams(
            collective_id=0, has_side_effects=True, vmem_limit_bytes=40 * 1024 * 1024
        ),
    )(gradient, feedback, warm_start, master, moment, second)
    right_factor = jnp.swapaxes(right, 1, 2).reshape(depth, rank)
    return (new_feedback, weights, master_out, moment_out, second_out, right_factor)


def solution(mesh):
    return jax.shard_map(
        on_device,
        mesh=mesh,
        in_specs=(
            P("rep", None, "shard"),
            P("rep", None, "shard"),
            P(),
            P("rep", "shard"),
            P("rep", "shard"),
            P("rep", "shard"),
        ),
        out_specs=(
            P("rep", None, "shard"),
            P(None, "shard"),
            P("rep", "shard"),
            P("rep", "shard"),
            P("rep", "shard"),
            P(),
        ),
        check_vma=False,
    )
```

```python
import functools

import jax
import jax.numpy as jnp
from jax import lax
from jax.experimental import pallas as pl
from jax.experimental.pallas import tpu as pltpu
from jax.sharding import PartitionSpec as P

HIGHEST = lax.Precision.HIGHEST
MESH = pl.DeviceIdType.MESH
beta_one = 0.9
beta_two = 0.95
learn_rate = 0.02
decay_rate = 0.1
adam_eps = 1e-08
ridge_rate = 1e-06
bf16 = jnp.bfloat16
f32 = jnp.float32


def lower_inverse(gram, order, width=4):
    rows = lax.broadcasted_iota(jnp.int32, (order, order), 0)
    cols = lax.broadcasted_iota(jnp.int32, (order, order), 1)
    eye = (rows == cols).astype(f32)
    trace = jnp.sum(gram * eye, keepdims=True)
    work = jnp.concatenate([gram + (ridge_rate / order) * trace * eye, eye], axis=1)
    done = []
    for top in range(0, order, 8):
        height = order - top
        below = lax.broadcasted_iota(jnp.int32, (height, 2 * order), 0)
        for first in range(0, 8, width):
            pick = range(first, first + width)
            c = {k: jnp.broadcast_to(work[:, top + k : top + k + 1], work.shape) for k in pick}
            r = {k: work[k : k + 1, :] for k in pick}
            s = {(i, k): c[k][i : i + 1, :] for k in pick for i in pick if i >= k}
            terms = []
            for k in pick:
                inv = 1.0 / s[k, k]
                later = range(k + 1, first + width)
                m = {i: s[i, k] * inv for i in later}
                column = c[k] * inv
                terms.append(jnp.where(below > k, column, 0.0) * r[k])
                for i in later:
                    for l in range(k + 1, i + 1):
                        s[i, l] = s[i, l] - m[i] * s[l, k]
                    c[i] = c[i] - column * s[i, k]
                    r[i] = r[i] - m[i] * r[k]
            for term in terms:
                work = work - term
        done.append(work[:8])
        work = work[8:]
    work = jnp.concatenate(done, axis=0)
    pivots = jnp.sum(work[:, :order] * eye, axis=1, keepdims=True)
    return work[:, order:] * (1.0 / jnp.sqrt(pivots))


def split(value):
    high = value.astype(bf16)
    return high, (value - high.astype(f32)).astype(bf16)


def nn(left, right):
    return jnp.dot(left, right, preferred_element_type=f32)


def nt(left, right, precision=None):
    return lax.dot_general(
        left, right, (((1,), (1,)), ((), ())), precision=precision, preferred_element_type=f32
    )


def kernel(
    reps, shards, inner, wide,
    g_hbm, f_hbm, w_ref, master_hbm, moment_hbm, second_hbm,
    nf_hbm, wt_hbm, apx_o, right_o,
    gv, fv, w2, ft, u3, rt, state, apx,
    fsend, frecv, fall, grams, psend, precv, qx, rall, wall,
    load_sem, state_sem, f_ss, f_rs, a_ss, a_rs, gr_ss, gr_rs, p_ss, p_rs, q_ss, q_rs, r_ss, r_rs,
    w_ss, w_rs, nf_sem, wo_sem, ao_sem, ro_sem,
):
    rank = w_ref.shape[0]
    depth, cols = gv.shape
    own_rows = state.shape[1]
    cb = fsend.shape[2]
    outer = reps // inner
    me = lax.axis_index("rep")
    ms = lax.axis_index("shard")
    groups = load_sem.shape[1]
    gw = cols // groups
    per = gw // cb

    def group(k, count, size):
        return lax.rem(lax.div(me, size) + 1 + k, count)

    def load(k):
        part = pl.ds(pl.multiple_of(group(k, groups, per) * gw, gw), gw)
        return (
            pltpu.make_async_copy(g_hbm.at[0, :, part], gv.at[:, part], load_sem.at[0, k]),
            pltpu.make_async_copy(f_hbm.at[0, :, part], fv.at[:, part], load_sem.at[1, k]),
        )

    for k in range(groups):
        for copy in load(k):
            copy.start()
    state_in = [
        pltpu.make_async_copy(src, state.at[i], state_sem.at[i])
        for i, src in enumerate((master_hbm, moment_hbm, second_hbm))
    ]
    for copy in state_in:
        copy.start()

    barrier = pltpu.get_barrier_semaphore()
    for k in range(1, reps):
        pl.semaphore_signal(barrier, inc=1, device_id={"rep": lax.rem(me + k, reps)}, device_id_type=MESH)
    for k in range(1, shards):
        pl.semaphore_signal(barrier, inc=1, device_id={"shard": lax.rem(ms + k, shards)}, device_id_type=MESH)

    def remote(src, dst, send_sem, recv_sem, axis, peer):
        return pltpu.make_async_remote_copy(
            src_ref=src, dst_ref=dst, send_sem=send_sem, recv_sem=recv_sem,
            device_id={axis: peer}, device_id_type=MESH,
        )

    wh, wl = split(w_ref[...])
    w2[...] = jnp.concatenate([wh, wl], axis=0)

    def scatter(src, dst, ss, rs, peer):
        k = lax.rem(peer - me + reps, reps)
        return remote(src.at[peer], dst.at[k], ss.at[k], rs.at[k], "rep", peer)

    def scatter_group(value, base, count, width, src, dst, ss, rs):
        for q in range(count):
            peer = base + q
            src[peer] = value[:, q * width : (q + 1) * width]

            @pl.when(peer != me)
            def _():
                scatter(src, dst, ss, rs, peer).start()

    def scatter_sum(src, dst, ss, rs):
        total = src[me]
        for k in range(1, reps):
            remote(src.at[me], dst.at[k], ss.at[k], rs.at[k], "rep", lax.rem(me + k, reps)).wait_recv()
            total = total + dst[k]
        return total

    for k in range(groups):
        for copy in load(k):
            copy.wait()
        part = pl.ds(pl.multiple_of(group(k, groups, per) * gw, gw), gw)
        both = nn(w2[...], gv[:, part]) + nn(w2[...], fv[:, part])
        if k == 0:
            pl.semaphore_wait(barrier, reps + shards - 2)
        scatter_group(
            both[:rank] + both[rank:], group(k, groups, per) * per, per, cb, fsend, frecv, f_ss, f_rs
        )

    fall[me] = scatter_sum(fsend, frecv, f_ss, f_rs) * (1.0 / reps)

    def gather(buf, ss, rs, axis, size, mine, k, sending):
        peer = lax.rem(mine + k, size) if sending else lax.rem(mine + size - k, size)
        slot = mine if sending else peer
        return remote(buf.at[slot], buf.at[slot], ss.at[k], rs.at[k], axis, lax.rem(mine + k, size))

    def start_gather(buf, ss, rs, axis, size, mine):
        for k in range(1, size):
            gather(buf, ss, rs, axis, size, mine, k, True).start()

    def wait_gather(buf, ss, rs, axis, size, mine):
        for k in range(1, size):
            gather(buf, ss, rs, axis, size, mine, k, False).wait_recv()

    start_gather(fall, a_ss, a_rs, "rep", reps, me)
    wait_gather(fall, a_ss, a_rs, "rep", reps, me)
    for r in range(reps):
        ft[:, pl.ds(r * cb, cb)] = fall[r]
    factor = ft[...]
    grams[ms] = nt(factor, factor, HIGHEST)
    start_gather(grams, gr_ss, gr_rs, "shard", shards, ms)
    wait_gather(grams, gr_ss, gr_rs, "shard", shards, ms)
    gram = grams[0]
    for s in range(1, shards):
        gram = gram + grams[s]
    inverse = lower_inverse(gram, rank)
    basis = jnp.dot(inverse, ft[...], precision=HIGHEST, preferred_element_type=f32)
    uh, ul = split(basis)
    u3[...] = jnp.concatenate([uh, ul, uh], axis=0)

    many = wide // own_rows
    for k in range(depth // wide):
        index = group(k, depth // wide, many)
        part = pl.ds(pl.multiple_of(index * wide, wide), wide)
        both = nt(u3[: 2 * rank, :], gv[part, :]) + nt(u3[: 2 * rank, :], fv[part, :])
        scatter_group(
            both[:rank] + both[rank:], index * many, many, own_rows, psend, precv, p_ss, p_rs
        )
    total = scatter_sum(psend, precv, p_ss, p_rs)
    qx[ms] = total
    start_gather(qx, q_ss, q_rs, "shard", shards, ms)
    wait_gather(qx, q_ss, q_rs, "shard", shards, ms)
    total = qx[0]
    for s in range(1, shards):
        total = total + qx[s]
    rall[me] = total * (1.0 / reps)
    start_gather(rall, r_ss, r_rs, "rep", reps, me)

    def approx_rows(r):
        rh, rl = split(rall[r].T)
        return nn(jnp.concatenate([rh, rh, rl], axis=1), u3[...])

    apx[...] = approx_rows(me)
    apx_copy = pltpu.make_async_copy(apx, apx_o, ao_sem)
    apx_copy.start()
    ma = lax.div(me, inner)
    mb = lax.rem(me, inner)
    half_rows = own_rows // 2
    has_up = ma + 1 < outer
    has_down = ma > 0

    def hop(block, half, way, peer):
        part = wall.at[block, pl.ds(half * half_rows, half_rows)]
        return remote(part, part, w_ss.at[block, half, way], w_rs.at[block, half], "rep", peer)

    def across(block, half):
        for j in range(1, inner):
            hop(block, half, 1 + j, ma * inner + lax.rem(mb + j, inner)).start()

    def along(block, half, up, down):
        if up:
            @pl.when(has_up)
            def _():
                hop(block, half, 0, me + inner).start()
        if down:
            @pl.when(has_down)
            def _():
                hop(block, half, 1, me - inner).start()

    def keep(block, half):
        part = pl.ds(pl.multiple_of(block * own_rows + half * half_rows, half_rows), half_rows)
        src = wall.at[block, pl.ds(half * half_rows, half_rows)]
        return pltpu.make_async_copy(src, wt_hbm.at[part], wo_sem.at[block, half])

    step_rows = 16
    for half in range(2):

        def adam(i, carry):
            part = pl.ds(pl.multiple_of(half * half_rows + i * step_rows, step_rows), step_rows)
            grad = apx[part, :]
            master = state[0, part, :]
            moment_out = beta_one * state[1, part, :] + (1.0 - beta_one) * grad
            second_out = beta_two * state[2, part, :] + (1.0 - beta_two) * grad * grad
            master_out = master - learn_rate * (
                moment_out / (jnp.sqrt(second_out) + adam_eps) + decay_rate * master
            )
            wall[me, part, :] = master_out.astype(bf16)
            return carry

        if half == 0:
            for copy in state_in:
                copy.wait()
        lax.fori_loop(0, half_rows // step_rows, adam, 0)
        along(me, half, True, True)
        across(me, half)
        keep(me, half).start()

    def pass_on(t, half):
        for a, up in ((ma - t, True), (ma + t, False)):
            @pl.when((a >= 0) & (a < outer))
            def _():
                block = a * inner + mb
                hop(block, half, 0, me).wait_recv()
                along(block, half, up, not up)
                if not (t == 1 and half == 1):
                    across(block, half)
                keep(block, half).start()

    if outer > 1:
        pass_on(1, 0)
        pass_on(1, 1)
    for j in range(1, inner):
        block = ma * inner + lax.rem(mb + j, inner)
        hop(block, 1, 0, me).wait_recv()
        along(block, 1, True, True)
        keep(block, 1).start()

    wait_gather(rall, r_ss, r_rs, "rep", reps, me)
    for r in range(reps):
        rt[:, pl.ds(r * own_rows, own_rows)] = rall[r]
    right_copy = pltpu.make_async_copy(rt, right_o, ro_sem)
    right_copy.start()

    def residue(r):
        part = pl.ds(pl.multiple_of(r * own_rows, own_rows), own_rows)
        return part, pltpu.make_async_copy(gv.at[part], nf_hbm.at[0, part], nf_sem.at[r])

    def feedback_rows(r, carry):
        part, copy = residue(r)
        merged = gv[part, :].astype(f32) + fv[part, :].astype(f32)
        gv[part, :] = (merged - approx_rows(r)).astype(bf16)
        copy.start()
        return carry

    lax.fori_loop(0, reps, feedback_rows, 0)

    for t in range(2, outer):
        for half in range(2):
            pass_on(t, half)

    for a in range(outer):
        for j in range(1, inner):
            block = a * inner + lax.rem(mb + j, inner)
            hop(block, 0, 0, me).wait_recv()
            keep(block, 0).start()

            @pl.when(a != ma)
            def _():
                hop(block, 1, 0, me).wait_recv()
                keep(block, 1).start()

    for k in range(1, reps):
        peer = lax.rem(me + k, reps)
        scatter(fsend, frecv, f_ss, f_rs, peer).wait_send()
        scatter(psend, precv, p_ss, p_rs, peer).wait_send()
        gather(fall, a_ss, a_rs, "rep", reps, me, k, True).wait_send()
        gather(rall, r_ss, r_rs, "rep", reps, me, k, True).wait_send()
    for k in range(1, shards):
        gather(grams, gr_ss, gr_rs, "shard", shards, ms, k, True).wait_send()
        gather(qx, q_ss, q_rs, "shard", shards, ms, k, True).wait_send()

    def sent(block, half, way):
        hop(block, half, way, me).wait_send()

    for a in range(outer):
        block = a * inner + mb
        for half in range(2):
            @pl.when((a <= ma) & has_up)
            def _():
                sent(block, half, 0)

            @pl.when((a >= ma) & has_down)
            def _():
                sent(block, half, 1)

            for j in range(1, inner):
                if half == 0:
                    sent(block, half, 1 + j)
                else:
                    @pl.when((a != ma - 1) & (a != ma + 1))
                    def _():
                        sent(block, half, 1 + j)

    for j in range(1, inner):
        block = ma * inner + lax.rem(mb + j, inner)

        @pl.when(has_up)
        def _():
            sent(block, 1, 0)

        @pl.when(has_down)
        def _():
            sent(block, 1, 1)

    apx_copy.wait()
    right_copy.wait()
    for r in range(reps):
        residue(r)[1].wait()
        keep(r, 0).wait()
        keep(r, 1).wait()


def on_device(gradient, feedback, warm_start, master, moment, second):
    reps = lax.axis_size("rep")
    shards = lax.axis_size("shard")
    inner = 2 if reps <= 8 else 8
    _, depth, cols = gradient.shape
    rank = warm_start.shape[1]
    own_rows = master.shape[0]
    cb = cols // reps
    wide = max(256, own_rows)
    groups = cols // max(256, cb)
    dma = pltpu.SemaphoreType.DMA
    anywhere = pl.BlockSpec(memory_space=pl.ANY)
    hbm = pl.BlockSpec(memory_space=pltpu.HBM)
    new_feedback, weights, grad_rows, right = pl.pallas_call(
        functools.partial(kernel, reps, shards, inner, wide),
        out_shape=(
            jax.ShapeDtypeStruct(gradient.shape, bf16),
            jax.ShapeDtypeStruct((depth, cols), bf16),
            jax.ShapeDtypeStruct(master.shape, f32),
            jax.ShapeDtypeStruct((rank, depth), f32),
        ),
        in_specs=[hbm, hbm, pl.BlockSpec(memory_space=pltpu.VMEM)] + [hbm] * 3,
        out_specs=(anywhere,) * 4,
        scratch_shapes=[
            pltpu.VMEM((depth, cols), bf16),
            pltpu.VMEM((depth, cols), bf16),
            pltpu.VMEM((2 * rank, depth), bf16),
            pltpu.VMEM((rank, cols), f32),
            pltpu.VMEM((3 * rank, cols), bf16),
            pltpu.VMEM((rank, depth), f32),
            pltpu.VMEM((3, own_rows, cols), f32),
            pltpu.VMEM((own_rows, cols), f32),
            pltpu.VMEM((reps, rank, cb), f32),
            pltpu.VMEM((reps, rank, cb), f32),
            pltpu.VMEM((reps, rank, cb), f32),
            pltpu.VMEM((shards, rank, rank), f32),
            pltpu.VMEM((reps, rank, own_rows), f32),
            pltpu.VMEM((reps, rank, own_rows), f32),
            pltpu.VMEM((shards, rank, own_rows), f32),
            pltpu.VMEM((reps, rank, own_rows), f32),
            pltpu.VMEM((reps, own_rows, cols), bf16),
            dma((2, groups)),
            dma((3,)),
            dma((reps,)), dma((reps,)),
            dma((reps,)), dma((reps,)),
            dma((shards,)), dma((shards,)),
            dma((reps,)), dma((reps,)),
            dma((shards,)), dma((shards,)),
            dma((reps,)), dma((reps,)),
            dma((reps, 2, inner + 1)), dma((reps, 2)),
            dma((reps,)), dma((reps, 2)), dma(()), dma(()),
        ],
        compiler_params=pltpu.CompilerParams(
            collective_id=0, has_side_effects=True, vmem_limit_bytes=60 * 1024 * 1024
        ),
    )(gradient, feedback, warm_start.T, master, moment, second)
    moment_out = beta_one * moment + (1.0 - beta_one) * grad_rows
    second_out = beta_two * second + (1.0 - beta_two) * grad_rows * grad_rows
    master_out = master - learn_rate * (
        moment_out / (jnp.sqrt(second_out) + adam_eps) + decay_rate * master
    )
    return (new_feedback, weights, master_out, moment_out, second_out, right.T)


def solution(mesh):
    return jax.shard_map(
        on_device,
        mesh=mesh,
        in_specs=(
            P("rep", None, "shard"),
            P("rep", None, "shard"),
            P(),
            P("rep", "shard"),
            P("rep", "shard"),
            P("rep", "shard"),
        ),
        out_specs=(
            P("rep", None, "shard"),
            P(None, "shard"),
            P("rep", "shard"),
            P("rep", "shard"),
            P("rep", "shard"),
            P(),
        ),
        check_vma=False,
    )
```

```python
import functools

import jax
import jax.numpy as jnp
from jax import lax
from jax.experimental import pallas as pl
from jax.experimental.pallas import tpu as pltpu
from jax.sharding import PartitionSpec as P

HIGHEST = lax.Precision.HIGHEST
MESH = pl.DeviceIdType.MESH
beta_one = 0.9
beta_two = 0.95
learn_rate = 0.02
decay_rate = 0.1
adam_eps = 1e-08
ridge_rate = 1e-06
bf16 = jnp.bfloat16
f32 = jnp.float32


def lower_inverse(gram, order, width=4):
    rows = lax.broadcasted_iota(jnp.int32, (order, order), 0)
    cols = lax.broadcasted_iota(jnp.int32, (order, order), 1)
    eye = (rows == cols).astype(f32)
    trace = jnp.sum(gram * eye, keepdims=True)
    work = jnp.concatenate([gram + (ridge_rate / order) * trace * eye, eye], axis=1)
    done = []
    for top in range(0, order, 8):
        height = order - top
        below = lax.broadcasted_iota(jnp.int32, (height, 2 * order), 0)
        for first in range(0, 8, width):
            pick = range(first, first + width)
            c = {k: jnp.broadcast_to(work[:, top + k : top + k + 1], work.shape) for k in pick}
            r = {k: work[k : k + 1, :] for k in pick}
            s = {(i, k): c[k][i : i + 1, :] for k in pick for i in pick if i >= k}
            terms = []
            for k in pick:
                inv = 1.0 / s[k, k]
                later = range(k + 1, first + width)
                m = {i: s[i, k] * inv for i in later}
                column = c[k] * inv
                terms.append(jnp.where(below > k, column, 0.0) * r[k])
                for i in later:
                    for l in range(k + 1, i + 1):
                        s[i, l] = s[i, l] - m[i] * s[l, k]
                    c[i] = c[i] - column * s[i, k]
                    r[i] = r[i] - m[i] * r[k]
            for term in terms:
                work = work - term
        done.append(work[:8])
        work = work[8:]
    work = jnp.concatenate(done, axis=0)
    pivots = jnp.sum(work[:, :order] * eye, axis=1, keepdims=True)
    return work[:, order:] * (1.0 / jnp.sqrt(pivots))


def split(value):
    high = value.astype(bf16)
    return high, (value - high.astype(f32)).astype(bf16)


def nn(left, right):
    return jnp.dot(left, right, preferred_element_type=f32)


def nt(left, right, precision=None):
    return lax.dot_general(
        left, right, (((1,), (1,)), ((), ())), precision=precision, preferred_element_type=f32
    )


def kernel(
    reps, shards, inner, wide,
    g_hbm, f_hbm, w_ref, master_hbm, moment_hbm, second_hbm,
    nf_hbm, wt_hbm, apx_o, right_o,
    gv, fv, w2, ft, u3, rt, state, apx,
    fsend, frecv, fall, grams, gramr, psend, precv, qx, rall, wall,
    load_sem, state_sem, f_ss, f_rs, a_ss, a_rs, gr_ss, gr_rs, gg_ss, gg_rs, p_ss, p_rs, q_ss, q_rs, r_ss, r_rs,
    w_ss, w_rs, nf_sem, wo_sem, ao_sem, ro_sem,
):
    rank = w_ref.shape[0]
    depth, cols = gv.shape
    own_rows = state.shape[1]
    cb = fsend.shape[2]
    outer = reps // inner
    me = lax.axis_index("rep")
    ms = lax.axis_index("shard")
    groups = load_sem.shape[1]
    gw = cols // groups
    per = gw // cb

    def group(k, count, size):
        return lax.rem(lax.div(me, size) + 1 + k, count)

    def load(k):
        part = pl.ds(pl.multiple_of(group(k, groups, per) * gw, gw), gw)
        return (
            pltpu.make_async_copy(g_hbm.at[0, :, part], gv.at[:, part], load_sem.at[0, k]),
            pltpu.make_async_copy(f_hbm.at[0, :, part], fv.at[:, part], load_sem.at[1, k]),
        )

    for k in range(groups):
        for copy in load(k):
            copy.start()
    state_in = [
        pltpu.make_async_copy(src, state.at[i], state_sem.at[i])
        for i, src in enumerate((master_hbm, moment_hbm, second_hbm))
    ]
    for copy in state_in:
        copy.start()

    barrier = pltpu.get_barrier_semaphore()
    for k in range(1, reps):
        pl.semaphore_signal(barrier, inc=1, device_id={"rep": lax.rem(me + k, reps)}, device_id_type=MESH)
    for k in range(1, shards):
        pl.semaphore_signal(barrier, inc=1, device_id={"shard": lax.rem(ms + k, shards)}, device_id_type=MESH)

    def remote(src, dst, send_sem, recv_sem, axis, peer):
        return pltpu.make_async_remote_copy(
            src_ref=src, dst_ref=dst, send_sem=send_sem, recv_sem=recv_sem,
            device_id={axis: peer}, device_id_type=MESH,
        )

    wh, wl = split(w_ref[...])
    w2[...] = jnp.concatenate([wh, wl], axis=0)

    def scatter(src, dst, ss, rs, peer):
        k = lax.rem(peer - me + reps, reps)
        return remote(src.at[peer], dst.at[k], ss.at[k], rs.at[k], "rep", peer)

    def scatter_group(value, base, count, width, src, dst, ss, rs):
        for q in range(count):
            peer = base + q
            src[peer] = value[:, q * width : (q + 1) * width]

            @pl.when(peer != me)
            def _():
                scatter(src, dst, ss, rs, peer).start()

    def scatter_sum(src, dst, ss, rs):
        total = src[me]
        for k in range(1, reps):
            remote(src.at[me], dst.at[k], ss.at[k], rs.at[k], "rep", lax.rem(me + k, reps)).wait_recv()
            total = total + dst[k]
        return total

    for k in range(groups):
        for copy in load(k):
            copy.wait()
        part = pl.ds(pl.multiple_of(group(k, groups, per) * gw, gw), gw)
        both = nn(w2[...], gv[:, part]) + nn(w2[...], fv[:, part])
        if k == 0:
            pl.semaphore_wait(barrier, reps + shards - 2)
        scatter_group(
            both[:rank] + both[rank:], group(k, groups, per) * per, per, cb, fsend, frecv, f_ss, f_rs
        )

    block = scatter_sum(fsend, frecv, f_ss, f_rs) * (1.0 / reps)
    fall[me] = block

    def gather(buf, ss, rs, axis, size, mine, k, sending):
        peer = lax.rem(mine + k, size) if sending else lax.rem(mine + size - k, size)
        slot = mine if sending else peer
        return remote(buf.at[slot], buf.at[slot], ss.at[k], rs.at[k], axis, lax.rem(mine + k, size))

    def start_gather(buf, ss, rs, axis, size, mine):
        for k in range(1, size):
            gather(buf, ss, rs, axis, size, mine, k, True).start()

    def wait_gather(buf, ss, rs, axis, size, mine):
        for k in range(1, size):
            gather(buf, ss, rs, axis, size, mine, k, False).wait_recv()

    half_rank = rank // 2
    terms = nt(block, block, HIGHEST)
    grams[ms] = jnp.concatenate([terms[:half_rank], terms[half_rank:]], axis=1)
    start_gather(grams, gr_ss, gr_rs, "shard", shards, ms)
    wait_gather(grams, gr_ss, gr_rs, "shard", shards, ms)
    packed = grams[0]
    for s in range(1, shards):
        packed = packed + grams[s]
    gramr[me] = packed
    start_gather(gramr, gg_ss, gg_rs, "rep", reps, me)
    start_gather(fall, a_ss, a_rs, "rep", reps, me)
    wait_gather(gramr, gg_ss, gg_rs, "rep", reps, me)
    packed = gramr[0]
    for r in range(1, reps):
        packed = packed + gramr[r]
    gram = jnp.concatenate([packed[:, :rank], packed[:, rank:]], axis=0)
    inverse = lower_inverse(gram, rank)
    wait_gather(fall, a_ss, a_rs, "rep", reps, me)
    for r in range(reps):
        ft[:, pl.ds(r * cb, cb)] = fall[r]
    basis = jnp.dot(inverse, ft[...], precision=HIGHEST, preferred_element_type=f32)
    uh, ul = split(basis)
    u3[...] = jnp.concatenate([uh, ul, uh], axis=0)

    many = wide // own_rows
    for k in range(depth // wide):
        index = group(k, depth // wide, many)
        part = pl.ds(pl.multiple_of(index * wide, wide), wide)
        both = nt(u3[: 2 * rank, :], gv[part, :]) + nt(u3[: 2 * rank, :], fv[part, :])
        scatter_group(
            both[:rank] + both[rank:], index * many, many, own_rows, psend, precv, p_ss, p_rs
        )
    total = scatter_sum(psend, precv, p_ss, p_rs)
    qx[ms] = total
    start_gather(qx, q_ss, q_rs, "shard", shards, ms)
    wait_gather(qx, q_ss, q_rs, "shard", shards, ms)
    total = qx[0]
    for s in range(1, shards):
        total = total + qx[s]
    rall[me] = total * (1.0 / reps)
    start_gather(rall, r_ss, r_rs, "rep", reps, me)

    def approx_rows(r):
        rh, rl = split(rall[r].T)
        return nn(jnp.concatenate([rh, rh, rl], axis=1), u3[...])

    apx[...] = approx_rows(me)
    apx_copy = pltpu.make_async_copy(apx, apx_o, ao_sem)
    apx_copy.start()
    ma = lax.div(me, inner)
    mb = lax.rem(me, inner)
    half_rows = own_rows // 2
    has_up = ma + 1 < outer
    has_down = ma > 0

    def hop(block, half, way, peer):
        part = wall.at[block, pl.ds(half * half_rows, half_rows)]
        return remote(part, part, w_ss.at[block, half, way], w_rs.at[block, half], "rep", peer)

    def across(block, half):
        for j in range(1, inner):
            hop(block, half, 1 + j, ma * inner + lax.rem(mb + j, inner)).start()

    def along(block, half, up, down):
        if up:
            @pl.when(has_up)
            def _():
                hop(block, half, 0, me + inner).start()
        if down:
            @pl.when(has_down)
            def _():
                hop(block, half, 1, me - inner).start()

    def keep(block, half):
        part = pl.ds(pl.multiple_of(block * own_rows + half * half_rows, half_rows), half_rows)
        src = wall.at[block, pl.ds(half * half_rows, half_rows)]
        return pltpu.make_async_copy(src, wt_hbm.at[part], wo_sem.at[block, half])

    step_rows = 16
    for half in range(2):

        def adam(i, carry):
            part = pl.ds(pl.multiple_of(half * half_rows + i * step_rows, step_rows), step_rows)
            grad = apx[part, :]
            master = state[0, part, :]
            moment_out = beta_one * state[1, part, :] + (1.0 - beta_one) * grad
            second_out = beta_two * state[2, part, :] + (1.0 - beta_two) * grad * grad
            master_out = master - learn_rate * (
                moment_out / (jnp.sqrt(second_out) + adam_eps) + decay_rate * master
            )
            wall[me, part, :] = master_out.astype(bf16)
            return carry

        if half == 0:
            for copy in state_in:
                copy.wait()
        lax.fori_loop(0, half_rows // step_rows, adam, 0)
        along(me, half, True, True)
        across(me, half)
        keep(me, half).start()

    def pass_on(t, half):
        for a, up in ((ma - t, True), (ma + t, False)):
            @pl.when((a >= 0) & (a < outer))
            def _():
                block = a * inner + mb
                hop(block, half, 0, me).wait_recv()
                along(block, half, up, not up)
                if not (t == 1 and half == 1):
                    across(block, half)
                keep(block, half).start()

    def residue(r):
        part = pl.ds(pl.multiple_of(r * own_rows, own_rows), own_rows)
        return part, pltpu.make_async_copy(gv.at[part], nf_hbm.at[0, part], nf_sem.at[r])

    def feedback_rows(r, carry):
        part, copy = residue(r)
        merged = gv[part, :].astype(f32) + fv[part, :].astype(f32)
        gv[part, :] = (merged - approx_rows(r)).astype(bf16)
        copy.start()
        return carry

    stages = 4

    def feedback(stage):
        lax.fori_loop(reps * stage // stages, reps * (stage + 1) // stages, feedback_rows, 0)

    if outer > 1:
        pass_on(1, 0)
    wait_gather(rall, r_ss, r_rs, "rep", reps, me)
    for r in range(reps):
        rt[:, pl.ds(r * own_rows, own_rows)] = rall[r]
    right_copy = pltpu.make_async_copy(rt, right_o, ro_sem)
    right_copy.start()
    feedback(0)
    if outer > 1:
        pass_on(1, 1)
    for j in range(1, inner):
        block = ma * inner + lax.rem(mb + j, inner)
        hop(block, 1, 0, me).wait_recv()
        along(block, 1, True, True)
        keep(block, 1).start()
    feedback(1)
    if outer > 2:
        pass_on(2, 0)
    feedback(2)
    if outer > 2:
        pass_on(2, 1)
    feedback(3)
    for t in range(3, outer):
        for half in range(2):
            pass_on(t, half)

    for a in range(outer):
        for j in range(1, inner):
            block = a * inner + lax.rem(mb + j, inner)
            hop(block, 0, 0, me).wait_recv()
            keep(block, 0).start()

            @pl.when(a != ma)
            def _():
                hop(block, 1, 0, me).wait_recv()
                keep(block, 1).start()

    for k in range(1, reps):
        peer = lax.rem(me + k, reps)
        scatter(fsend, frecv, f_ss, f_rs, peer).wait_send()
        scatter(psend, precv, p_ss, p_rs, peer).wait_send()
        gather(fall, a_ss, a_rs, "rep", reps, me, k, True).wait_send()
        gather(rall, r_ss, r_rs, "rep", reps, me, k, True).wait_send()
        gather(gramr, gg_ss, gg_rs, "rep", reps, me, k, True).wait_send()
    for k in range(1, shards):
        gather(grams, gr_ss, gr_rs, "shard", shards, ms, k, True).wait_send()
        gather(qx, q_ss, q_rs, "shard", shards, ms, k, True).wait_send()

    def sent(block, half, way):
        hop(block, half, way, me).wait_send()

    for a in range(outer):
        block = a * inner + mb
        for half in range(2):
            @pl.when((a <= ma) & has_up)
            def _():
                sent(block, half, 0)

            @pl.when((a >= ma) & has_down)
            def _():
                sent(block, half, 1)

            for j in range(1, inner):
                if half == 0:
                    sent(block, half, 1 + j)
                else:
                    @pl.when((a != ma - 1) & (a != ma + 1))
                    def _():
                        sent(block, half, 1 + j)

    for j in range(1, inner):
        block = ma * inner + lax.rem(mb + j, inner)

        @pl.when(has_up)
        def _():
            sent(block, 1, 0)

        @pl.when(has_down)
        def _():
            sent(block, 1, 1)

    apx_copy.wait()
    right_copy.wait()
    for r in range(reps):
        residue(r)[1].wait()
        keep(r, 0).wait()
        keep(r, 1).wait()


def finish(
    nf_i, wt_i, right_i, apx, master, moment, second,
    nf_o, wt_o, right_o, master_o, moment_o, second_o,
    grad_v, state, big_sem, right_sem, in_sem, out_sem,
):
    pieces = in_sem.shape[1]
    rows = grad_v.shape[0] // pieces
    depth = wt_i.shape[0]
    big = depth // big_sem.shape[1]

    def load(p):
        part = pl.ds(p * rows, rows)
        into = (grad_v.at[part], state.at[0, part], state.at[1, part], state.at[2, part])
        return [
            pltpu.make_async_copy(src.at[part], dst, in_sem.at[i, p])
            for i, (src, dst) in enumerate(zip((apx, master, moment, second), into))
        ]

    def store(p):
        part = pl.ds(p * rows, rows)
        return [
            pltpu.make_async_copy(state.at[i, part], dst.at[part], out_sem.at[i, p])
            for i, dst in enumerate((master_o, moment_o, second_o))
        ]

    moves = [pltpu.make_async_copy(right_i, right_o, right_sem)]
    for p in range(big_sem.shape[1]):
        part = pl.ds(p * big, big)
        moves.append(pltpu.make_async_copy(nf_i.at[0, part], nf_o.at[0, part], big_sem.at[0, p]))
        moves.append(pltpu.make_async_copy(wt_i.at[part], wt_o.at[part], big_sem.at[1, p]))
    for p in range(pieces):
        for copy in load(p):
            copy.start()
    for copy in moves:
        copy.start()
    for p in range(pieces):
        for copy in load(p):
            copy.wait()
        part = pl.ds(p * rows, rows)
        grad = grad_v[part, :]
        master_in = state[0, part, :]
        moment_out = beta_one * state[1, part, :] + (1.0 - beta_one) * grad
        second_out = beta_two * state[2, part, :] + (1.0 - beta_two) * grad * grad
        state[0, part, :] = master_in - learn_rate * (
            moment_out / (jnp.sqrt(second_out) + adam_eps) + decay_rate * master_in
        )
        state[1, part, :] = moment_out
        state[2, part, :] = second_out
        for copy in store(p):
            copy.start()
    for p in range(pieces):
        for copy in store(p):
            copy.wait()
    for copy in moves:
        copy.wait()


def on_device(gradient, feedback, warm_start, master, moment, second):
    reps = lax.axis_size("rep")
    shards = lax.axis_size("shard")
    inner = 2 if reps <= 8 else 8
    _, depth, cols = gradient.shape
    rank = warm_start.shape[1]
    own_rows = master.shape[0]
    cb = cols // reps
    wide = max(256, own_rows)
    groups = cols // max(256, cb)
    dma = pltpu.SemaphoreType.DMA
    anywhere = pl.BlockSpec(memory_space=pl.ANY)
    hbm = pl.BlockSpec(memory_space=pltpu.HBM)
    new_feedback, weights, grad_rows, right = pl.pallas_call(
        functools.partial(kernel, reps, shards, inner, wide),
        out_shape=(
            jax.ShapeDtypeStruct(gradient.shape, bf16),
            jax.ShapeDtypeStruct((depth, cols), bf16),
            jax.ShapeDtypeStruct(master.shape, f32),
            jax.ShapeDtypeStruct((rank, depth), f32),
        ),
        in_specs=[hbm, hbm, pl.BlockSpec(memory_space=pltpu.VMEM)] + [hbm] * 3,
        out_specs=(anywhere,) * 4,
        scratch_shapes=[
            pltpu.VMEM((depth, cols), bf16),
            pltpu.VMEM((depth, cols), bf16),
            pltpu.VMEM((2 * rank, depth), bf16),
            pltpu.VMEM((rank, cols), f32),
            pltpu.VMEM((3 * rank, cols), bf16),
            pltpu.VMEM((rank, depth), f32),
            pltpu.VMEM((3, own_rows, cols), f32),
            pltpu.VMEM((own_rows, cols), f32),
            pltpu.VMEM((reps, rank, cb), f32),
            pltpu.VMEM((reps, rank, cb), f32),
            pltpu.VMEM((reps, rank, cb), f32),
            pltpu.VMEM((shards, rank // 2, 2 * rank), f32),
            pltpu.VMEM((reps, rank // 2, 2 * rank), f32),
            pltpu.VMEM((reps, rank, own_rows), f32),
            pltpu.VMEM((reps, rank, own_rows), f32),
            pltpu.VMEM((shards, rank, own_rows), f32),
            pltpu.VMEM((reps, rank, own_rows), f32),
            pltpu.VMEM((reps, own_rows, cols), bf16),
            dma((2, groups)),
            dma((3,)),
            dma((reps,)), dma((reps,)),
            dma((reps,)), dma((reps,)),
            dma((shards,)), dma((shards,)),
            dma((reps,)), dma((reps,)),
            dma((reps,)), dma((reps,)),
            dma((shards,)), dma((shards,)),
            dma((reps,)), dma((reps,)),
            dma((reps, 2, inner + 1)), dma((reps, 2)),
            dma((reps,)), dma((reps, 2)), dma(()), dma(()),
        ],
        compiler_params=pltpu.CompilerParams(
            collective_id=0, has_side_effects=True, vmem_limit_bytes=60 * 1024 * 1024
        ),
    )(gradient, feedback, warm_start.T, master, moment, second)
    pieces, moves = 4, 8
    new_feedback, weights, right, master_out, moment_out, second_out = pl.pallas_call(
        finish,
        out_shape=(
            jax.ShapeDtypeStruct(gradient.shape, bf16),
            jax.ShapeDtypeStruct((depth, cols), bf16),
            jax.ShapeDtypeStruct((rank, depth), f32),
            jax.ShapeDtypeStruct(master.shape, f32),
            jax.ShapeDtypeStruct(master.shape, f32),
            jax.ShapeDtypeStruct(master.shape, f32),
        ),
        in_specs=[hbm] * 7,
        out_specs=(hbm,) * 6,
        scratch_shapes=[
            pltpu.VMEM((own_rows, cols), f32),
            pltpu.VMEM((3, own_rows, cols), f32),
            dma((2, moves)), dma(()), dma((4, pieces)), dma((3, pieces)),
        ],
        compiler_params=pltpu.CompilerParams(vmem_limit_bytes=60 * 1024 * 1024),
    )(new_feedback, weights, right, grad_rows, master, moment, second)
    return (new_feedback, weights, master_out, moment_out, second_out, right.T)


def solution(mesh):
    return jax.shard_map(
        on_device,
        mesh=mesh,
        in_specs=(
            P("rep", None, "shard"),
            P("rep", None, "shard"),
            P(),
            P("rep", "shard"),
            P("rep", "shard"),
            P("rep", "shard"),
        ),
        out_specs=(
            P("rep", None, "shard"),
            P(None, "shard"),
            P("rep", "shard"),
            P("rep", "shard"),
            P("rep", "shard"),
            P(),
        ),
        check_vma=False,
    )
```
